32 devices in a mesh: pair: 16 (over z, y, x), vir: 2 (over core).
Axes of the slice: x: 2, y: 2, z: 4, core: 2. Of those that a mesh axis runs over, the one named last changes fastest.
Arguments:
- amplitudes: bfloat16 [40960, 1024], P('pair', 'vir'), may hold values from -6 to 6
- cycle_ints: bfloat16 [40960, 1024], P('pair', 'vir'), may hold values from -6 to 6
- int_rows: bfloat16 [1024, 1024], P('pair', 'vir'), may hold values from -6 to 6
- row_dest: int32 [1024, 2], P('pair'), may hold values from 0 to 15, all different within a row; in each aligned block of 64 rows (0 to 63, 64 to 127, ...) at most 16 rows name the same one
- vir_energy: float32 [1024], P('vir'), may hold values from 0.5 to 4
- occ_energy: float32 [40960], P('pair'), may hold values from -2 to -0.2
Outputs:
- residual: bfloat16 [40960, 1024], P('pair', 'vir')
The draws below stay inside these ranges and needn't reach their ends.
Inputs may be any that keep to these rules, and one draw needn't show every extreme that they name: `row_dest`: each integral row names 2 different pair groups; among the 64 rows of one pair group no group is named more than 16 times, a bound that some block reaches.
All inputs are finite; a program needn't handle non-finite values.
Results may differ from the reference program's by a relative error of at most 0.008.
Values may be sent and summed in bfloat16 or wider, within the bound.
A program may use at most 64 MiB of HBM per device.

```python
import math
import jax
import jax.numpy as jnp
import numpy as np
from jax import lax

NV = 1024
ROWS = 2560
R_DEV = 64
TOP = 2
SLOTS = 256
NPR = 40960
NR = 1024
N_PAIR = 16


def steps_of(rng, shape, cuts, least, high):
    factor_of, own = 1.0, jax.random.fold_in(rng, 6)
    for axis_at, shards_of in cuts:
        heights = jnp.exp(jax.random.uniform(jax.random.fold_in(own, axis_at), (shards_of,), jnp.float32, least / len(cuts), high / len(cuts)))
        factor_of = factor_of * jnp.repeat(heights, shape[axis_at] // shards_of).reshape([-1 if axis == axis_at else 1 for axis in range(len(shape))])
    return factor_of


def shared_out(own_key, own, number, rows, number_of, top, most, slope):
    order = jax.random.permutation(own_key, number_of)
    crowded, ordinary = load_shares(number_of, rows * top, most, slope, True), load_shares(number_of, rows * top, most, slope, False)
    places = jnp.arange(number_of)

    def named(sizes, rotation):
        used = int((sizes > 0).sum())
        fixed = max(1, used // 4)
        passed = fixed + (places - fixed + rotation * (used - fixed)) % max(1, number_of - fixed)
        return jnp.zeros((number_of,), jnp.int32).at[order[jnp.where(places < fixed, places, passed)]].set(jnp.asarray(sizes, jnp.int32))

    sizes = jnp.where(number % 4 == 0, named(crowded, number // 4), named(ordinary, number - number // 4 - 1))
    mixed = jax.random.permutation(jax.random.fold_in(own, 3), number_of)
    giver, receiver = mixed[0:number_of // 2 * 2:2], mixed[1:number_of // 2 * 2:2]
    room = jnp.minimum(sizes[giver] - 1, most - sizes[receiver]) // 2
    room = jnp.where((giver == order[0]) | (receiver == order[0]) | (sizes[receiver] == 0), 0, jnp.maximum(room, 0))
    passed = jax.random.randint(jax.random.fold_in(own, 4), (number_of // 2,), 0, 1 << 20) % (room + 1)
    sizes = sizes.at[giver].add(-passed).at[receiver].add(passed)
    labels = jnp.searchsorted(jnp.cumsum(sizes), jnp.arange(rows * top), side="right").astype(jnp.int32)
    grid = labels.reshape(top, rows).T
    grid = grid[jax.random.permutation(jax.random.fold_in(own, 1), rows)]
    rotation = jax.random.randint(jax.random.fold_in(own, 2), (rows, 1), 0, top)
    return jnp.take_along_axis(grid, (jnp.arange(top)[None, :] + rotation) % top, axis=1)


def load_shares(count, total, most, slope, full):
    weights = [(1 << 20) // math.isqrt(grade ** slope) + 1 for grade in range(1, count + 1)]
    largest = most if full else min(most, max(-(-total // count), total * weights[0] // sum(weights)))
    least = 1 if total - largest >= count - 1 else 0
    holding, spare = [largest] + [least] * (count - 1), total - largest - least * (count - 1)
    while spare > 0:
        candidates = [i for i in range(1, count) if holding[i] < largest] or [i for i in range(1, count) if holding[i] < most]
        mass, left = sum([weights[i] for i in candidates]), spare
        for i in candidates:
            more = min(most - holding[i], max(1, left * weights[i] // mass), spare)
            holding[i] = holding[i] + more
            spare = spare - more
    return np.array(holding)


def gaussian(rng, extent, width, limit, cuts=(), held_as=jnp.bfloat16):
    values = width * jax.random.normal(rng, extent, jnp.float32)
    if cuts:
        values = values * steps_of(rng, extent, cuts, -0.22, 0.18)
    return jnp.clip(values, -limit, limit).astype(held_as)


def setup_inputs(seed: int = 0) -> dict:
    splits = jax.random.split(jax.random.key(seed), 7)
    amplitudes = gaussian(splits[0], (NPR, NV), 1.0, 6.0, ((0, 16), (1, 2)))
    cycle_ints = gaussian(splits[1], (NPR, NV), 1.0, 6.0, ((0, 16), (1, 2)))
    int_rows = gaussian(splits[2], (NR, NV), 1.0, 6.0, ((0, 16), (1, 2)))
    row_dest_keys = jax.random.split(jax.random.fold_in(splits[3], 1), NR // R_DEV)
    row_dest_turns = jax.random.permutation(jax.random.fold_in(splits[3], 3), NR // R_DEV)
    row_dest = jax.vmap(lambda own, number: shared_out(jax.random.fold_in(splits[3], 2), own, number, R_DEV, N_PAIR, TOP, SLOTS // N_PAIR, 2))(row_dest_keys, row_dest_turns).reshape((NR, TOP))
    vir_energy = jnp.clip(jnp.exp(math.log(4.0) - 2.0794415 * jax.random.uniform(splits[4], (NV,), jnp.float32) ** steps_of(splits[4], (NV,), ((0, 2),), -0.2, 0.2)), 0.5, 4.0)
    occ_energy = jnp.clip(-2.0 + 1.8 * jax.random.uniform(splits[5], (NPR,), jnp.float32) ** steps_of(splits[5], (NPR,), ((0, 16),), -0.2, 0.2), -2.0, -0.2)
    return {"amplitudes": amplitudes, "cycle_ints": cycle_ints, "int_rows": int_rows, "row_dest": row_dest, "vir_energy": vir_energy, "occ_energy": occ_energy}


def reference(amplitudes, cycle_ints, int_rows, row_dest, vir_energy, occ_energy):
    total_rows = ROWS * N_PAIR
    cross_sum = lax.dot_general(amplitudes, cycle_ints, (((0,), (0,)), ((), ())), preferred_element_type=jnp.float32)
    cross_sum = cross_sum / math.sqrt(total_rows * NV)
    cycle_term = jnp.dot(amplitudes, cross_sum.astype(jnp.bfloat16), preferred_element_type=jnp.float32)
    padded_rows = jnp.concatenate([int_rows, jnp.zeros((1, NV), int_rows.dtype)], axis=0)
    blocks = amplitudes.reshape(N_PAIR, ROWS, NV)

    def ladder_block(group_id):
        amp_block = blocks[group_id]
        routed = jnp.any(row_dest == group_id, axis=1)
        picked = jnp.nonzero(routed, size=SLOTS, fill_value=R_DEV * N_PAIR)[0].astype(jnp.int32)
        chosen = padded_rows[picked]
        coefficient = lax.dot_general(amp_block, chosen, (((1,), (1,)), ((), ())), preferred_element_type=jnp.float32)
        coefficient = coefficient / math.sqrt(NV)
        return jnp.dot(coefficient.astype(jnp.bfloat16), chosen, preferred_element_type=jnp.float32) / math.sqrt(SLOTS)
    ladder = lax.map(ladder_block, jnp.arange(N_PAIR, dtype=jnp.int32)).reshape(total_rows, NV)
    energy = (vir_energy[None, :] - occ_energy[:, None]) * amplitudes.astype(jnp.float32)
    return (cycle_term + ladder + energy).astype(jnp.bfloat16)
```

```python
import math

import jax
import jax.numpy as jnp
from jax import lax
from jax.sharding import PartitionSpec as P

SLOTS = 256


def dispatch(int_rows, row_dest, groups, capacity):
    rows = int_rows.shape[0]
    group = jnp.arange(groups, dtype=jnp.int32)
    member = jnp.any(row_dest[None, :, :] == group[:, None, None], axis=2)
    before = jnp.arange(rows)[:, None] < jnp.arange(rows)[None, :]
    rank = jnp.dot(
        member.astype(jnp.bfloat16), before.astype(jnp.bfloat16), preferred_element_type=jnp.float32
    ).astype(jnp.int32)
    slot = jnp.arange(capacity, dtype=jnp.int32)
    select = member[:, None, :] & (rank[:, None, :] == slot[None, :, None])
    select = select.reshape(groups * capacity, rows).astype(int_rows.dtype)
    return jnp.dot(select, int_rows, preferred_element_type=jnp.float32).astype(int_rows.dtype)


def body(amplitudes, cycle_ints, int_rows, row_dest, vir_energy, occ_energy):
    groups = lax.axis_size("pair")
    row_count, local_width = amplitudes.shape
    full_width = local_width * lax.axis_size("vir")
    capacity = SLOTS // groups
    gathered = lax.all_gather(amplitudes, "vir", axis=1, tiled=True)
    cross_part = lax.dot_general(
        gathered, cycle_ints, (((0,), (0,)), ((), ())), preferred_element_type=jnp.float32
    )
    scale_cycle = math.sqrt(row_count * groups * full_width)
    cross_half = lax.psum((cross_part / scale_cycle).astype(jnp.bfloat16), "pair")
    outgoing = dispatch(int_rows, row_dest, groups, capacity)
    arrived = lax.all_to_all(
        outgoing.reshape(groups, capacity, local_width),
        "pair",
        split_axis=0,
        concat_axis=0,
        tiled=True,
    ).reshape(groups * capacity, local_width)
    chosen = lax.all_gather(arrived, "vir", axis=1, tiled=True)
    coefficient = lax.dot_general(
        gathered, chosen, (((1,), (1,)), ((), ())), preferred_element_type=jnp.float32
    ) / math.sqrt(full_width)
    ladder = jnp.dot(
        coefficient.astype(jnp.bfloat16), arrived, preferred_element_type=jnp.float32
    ) / math.sqrt(SLOTS)
    energy = (vir_energy[None, :] - occ_energy[:, None]) * amplitudes.astype(jnp.float32)
    cycle_term = jnp.dot(gathered, cross_half, preferred_element_type=jnp.float32)
    return (cycle_term + ladder + energy).astype(jnp.bfloat16)


def solution(mesh):
    return jax.shard_map(
        body,
        mesh=mesh,
        in_specs=(
            P("pair", "vir"),
            P("pair", "vir"),
            P("pair", "vir"),
            P("pair", None),
            P("vir"),
            P("pair"),
        ),
        out_specs=P("pair", "vir"),
        check_vma=False,
    )
```

```python
import math

import jax
import jax.numpy as jnp
from jax import lax
from jax.experimental import pallas as pl
from jax.experimental.pallas import tpu as pltpu
from jax.sharding import PartitionSpec as P

SLOTS = 256


def dispatch(int_rows, row_dest, groups, capacity):
    rows = int_rows.shape[0]
    group = jnp.arange(groups, dtype=jnp.int32)
    member = jnp.any(row_dest[None, :, :] == group[:, None, None], axis=2)
    before = jnp.arange(rows)[:, None] < jnp.arange(rows)[None, :]
    rank = jnp.dot(
        member.astype(jnp.bfloat16), before.astype(jnp.bfloat16), preferred_element_type=jnp.float32
    ).astype(jnp.int32)
    slot = jnp.arange(capacity, dtype=jnp.int32)
    select = member[:, None, :] & (rank[:, None, :] == slot[None, :, None])
    select = select.reshape(groups * capacity, rows).astype(int_rows.dtype)
    return jnp.dot(select, int_rows, preferred_element_type=jnp.float32).astype(int_rows.dtype)


def body(amplitudes, cycle_ints, int_rows, row_dest, vir_energy, occ_energy):
    groups = lax.axis_size("pair")
    row_count, local_width = amplitudes.shape
    full_width = local_width * lax.axis_size("vir")
    capacity = SLOTS // groups
    gathered = lax.all_gather(amplitudes, "vir", axis=1, tiled=True)
    cross_part = lax.dot_general(
        gathered, cycle_ints, (((0,), (0,)), ((), ())), preferred_element_type=jnp.float32
    )
    scale_cycle = math.sqrt(row_count * groups * full_width)
    cross_half = lax.psum((cross_part / scale_cycle).astype(jnp.bfloat16), "pair")
    outgoing = dispatch(int_rows, row_dest, groups, capacity)
    arrived = lax.all_to_all(
        outgoing.reshape(groups, capacity, local_width),
        "pair",
        split_axis=0,
        concat_axis=0,
        tiled=True,
    ).reshape(groups * capacity, local_width)
    chosen = lax.all_gather(arrived, "vir", axis=1, tiled=True)
    coefficient = lax.dot_general(
        gathered, chosen, (((1,), (1,)), ((), ())), preferred_element_type=jnp.float32
    ) / math.sqrt(full_width)
    ladder = jnp.dot(
        coefficient.astype(jnp.bfloat16), arrived, preferred_element_type=jnp.float32
    ) / math.sqrt(SLOTS)
    energy = (vir_energy[None, :] - occ_energy[:, None]) * amplitudes.astype(jnp.float32)
    cycle_term = jnp.dot(gathered, cross_half, preferred_element_type=jnp.float32)
    return (cycle_term + ladder + energy).astype(jnp.bfloat16)


DEPTH, PLANE, HALVES, PIECES = 4, 4, 2, 4
F32, BF16 = jnp.float32, jnp.bfloat16


def rows_at(start, size):
    return pl.ds(pl.multiple_of(start, size), size)


def kernel(
    amp, cyc, rows, dest, vir_e, occ_e, out,
    other, part, plane_in, zsum, z_in, full, outgoing, arr, arr_o, acc,
    amp_sem, route_sem, arr_sem, plane_sem, z_sem, gz_sem, gp_sem,
):
    groups = DEPTH * PLANE
    me, v = lax.axis_index("pair"), lax.axis_index("vir")
    z, q = me // PLANE, me % PLANE
    count, width = amp.shape
    full_width = 2 * width
    capacity = SLOTS // groups
    half = width // HALVES
    block = full_width // PLANE
    piece = block // DEPTH

    barrier = pltpu.get_barrier_semaphore()
    for k in range(1, groups):
        pl.semaphore_signal(
            barrier, inc=1, device_id=((me + k) % groups, v), device_id_type=pl.DeviceIdType.MESH
        )
    pl.semaphore_signal(barrier, inc=1, device_id=(me, 1 - v), device_id_type=pl.DeviceIdType.MESH)

    def copy(src, dst, sem, index, device):
        return pltpu.make_async_remote_copy(
            src_ref=src,
            dst_ref=dst,
            send_sem=sem.at[(0, *index)],
            recv_sem=sem.at[(1, *index)],
            device_id=device,
            device_id_type=pl.DeviceIdType.MESH,
        )

    group = lax.broadcasted_iota(jnp.int32, (SLOTS, rows.shape[0]), 0) // capacity
    slot = lax.broadcasted_iota(jnp.int32, (SLOTS, rows.shape[0]), 0) % capacity
    member = group == dest[0:1, :]
    for k in range(1, dest.shape[0]):
        member = member | (group == dest[k : k + 1, :])
    tri = (rows.shape[0], rows.shape[0])
    before = lax.broadcasted_iota(jnp.int32, tri, 0) < lax.broadcasted_iota(jnp.int32, tri, 1)
    rank = jnp.dot(
        jnp.where(member, 1.0, 0.0).astype(BF16),
        jnp.where(before, 1.0, 0.0).astype(BF16),
        preferred_element_type=F32,
    )
    select = jnp.where(member & (rank == slot.astype(F32)), 1.0, 0.0).astype(BF16)
    outgoing[...] = jnp.dot(select, rows[...], preferred_element_type=F32).astype(BF16)
    pl.semaphore_wait(barrier, groups)

    step = count // PIECES
    amp_copies = [
        copy(amp.at[pl.ds(i * step, step)], other.at[pl.ds(i * step, step)], amp_sem, (i,), (me, 1 - v))
        for i in range(PIECES)
    ]
    for c in amp_copies:
        c.start()
    route_copies = []
    for k in range(1, groups):
        to = (me + k) % groups
        c = copy(
            outgoing.at[rows_at(to * capacity, capacity)],
            arr.at[rows_at(me * capacity, capacity)],
            route_sem, (k - 1,), (to, v),
        )
        c.start()
        route_copies.append(c)
    mine = rows_at(me * capacity, capacity)
    arr[mine, :] = outgoing[mine, :]

    plane_copies = [
        [
            copy(
                part.at[h, rows_at((q + d) % PLANE * block, block)],
                plane_in.at[h, d - 1],
                plane_sem, (h, d - 1), (z * PLANE + (q + d) % PLANE, v),
            )
            for d in range(1, PLANE)
        ]
        for h in range(HALVES)
    ]

    def cross(src, owner, h):
        for j in range(width // block):
            value = lax.dot_general(
                src[:, pl.ds(j * block, block)],
                cyc[:, pl.ds(h * half, half)],
                (((0,), (0,)), ((), ())),
                preferred_element_type=F32,
            )
            part[h, rows_at(owner * width + j * block, block), :] = value.astype(BF16)
        for d in range(1, PLANE):
            target = (q + d) % PLANE

            @pl.when(target // (PLANE // 2) == owner)
            def _():
                plane_copies[h][d - 1].start()

    for h in range(HALVES):
        cross(amp, v, h)
    for c in route_copies:
        c.wait_recv()
    arr_copy = copy(arr, arr_o, arr_sem, (0,), (me, 1 - v))
    arr_copy.start()
    for c in amp_copies:
        c.wait_recv()
    for h in range(HALVES):
        cross(other, 1 - v, h)
    arr_copy.wait_recv()

    tile = 256
    contract = (((1,), (1,)), ((), ()))

    def ladder(t, carry):
        at = rows_at(t * tile, tile)
        mine = amp[at, :]
        value = lax.dot_general(mine, arr[...], contract, preferred_element_type=F32)
        value += lax.dot_general(other[at, :], arr_o[...], contract, preferred_element_type=F32)
        value = (value / math.sqrt(full_width)).astype(BF16)
        value = jnp.dot(value, arr[...], preferred_element_type=F32) / math.sqrt(SLOTS)
        for s in range(tile // 128):
            line = jnp.broadcast_to(occ_e[pl.ds(t * (tile // 128) + s, 1), :], (128, 128)).T
            for b in range(width // 128):
                cols = slice(b * 128, (b + 1) * 128)
                sub = slice(s * 128, (s + 1) * 128)
                acc[pl.ds(pl.multiple_of(t * tile + s * 128, 128), 128), cols] = value[sub, cols] + (
                    vir_e[:, cols] - line
                ) * mine[sub, cols].astype(F32)
        return carry

    tiles = count // tile
    z_copies, gz_copies, gp_copies = [], [], []
    for h in range(HALVES):
        lax.fori_loop(h * tiles // HALVES, (h + 1) * tiles // HALVES, ladder, 0)
        for c in plane_copies[h]:
            c.wait_recv()
        total = part[h, rows_at(q * block, block), :].astype(F32)
        for d in range(1, PLANE):
            total += plane_in[h, d - 1].astype(F32)
        zsum[h] = total.astype(BF16)
        for e in range(1, DEPTH):
            to = (z + e) % DEPTH
            c = copy(
                zsum.at[h, rows_at(to * piece, piece)],
                z_in.at[h, e - 1],
                z_sem, (h, e - 1), (to * PLANE + q, v),
            )
            c.start()
            z_copies.append(c)
    scale = math.sqrt(count * groups * full_width)
    own = rows_at((q * DEPTH + z) * piece, piece)
    for h in range(HALVES):
        for e in range(1, DEPTH):
            z_copies[h * (DEPTH - 1) + e - 1].wait_recv()
        total = zsum[h, rows_at(z * piece, piece), :].astype(F32)
        for e in range(1, DEPTH):
            total += z_in[h, e - 1].astype(F32)
        full[h, own, :] = (total / scale).astype(BF16)
        for e in range(1, DEPTH):
            c = copy(
                full.at[h, own], full.at[h, own], gz_sem, (h, e - 1), ((z + e) % DEPTH * PLANE + q, v)
            )
            c.start()
            gz_copies.append(c)
    whole = rows_at(q * block, block)
    for h in range(HALVES):
        for e in range(1, DEPTH):
            gz_copies[h * (DEPTH - 1) + e - 1].wait_recv()
        for d in range(1, PLANE):
            c = copy(
                full.at[h, whole], full.at[h, whole],
                gp_sem, (h, d - 1), (z * PLANE + (q + d) % PLANE, v),
            )
            c.start()
            gp_copies.append(c)
    for h in range(HALVES):
        for d in range(1, PLANE):
            gp_copies[h * (PLANE - 1) + d - 1].wait_recv()
        cols = slice(h * half, (h + 1) * half)

        def cycle(t, carry):
            at = rows_at(t * tile, tile)
            value = jnp.dot(
                amp[at, :], full[h, rows_at(v * width, width), :], preferred_element_type=F32
            )
            value += jnp.dot(
                other[at, :], full[h, rows_at((1 - v) * width, width), :], preferred_element_type=F32
            )
            out[at, cols] = (value + acc[at, cols]).astype(BF16)
            return carry

        lax.fori_loop(0, tiles, cycle, 0)
    plane_all = [c for part_of in plane_copies for c in part_of]
    for c in amp_copies + route_copies + [arr_copy] + plane_all + z_copies + gz_copies + gp_copies:
        c.wait_send()


def fused(amplitudes, cycle_ints, int_rows, row_dest, vir_energy, occ_energy):
    count, width = amplitudes.shape
    groups = DEPTH * PLANE
    half, block = width // HALVES, 2 * width // PLANE
    dma = pltpu.SemaphoreType.DMA
    return pl.pallas_call(
        kernel,
        out_shape=jax.ShapeDtypeStruct((count, width), BF16),
        in_specs=[pl.BlockSpec(memory_space=pltpu.VMEM)] * 6,
        out_specs=pl.BlockSpec(memory_space=pltpu.VMEM),
        scratch_shapes=[
            pltpu.VMEM((count, width), BF16),
            pltpu.VMEM((HALVES, 2 * width, half), BF16),
            pltpu.VMEM((HALVES, PLANE - 1, block, half), BF16),
            pltpu.VMEM((HALVES, block, half), BF16),
            pltpu.VMEM((HALVES, DEPTH - 1, block // DEPTH, half), BF16),
            pltpu.VMEM((HALVES, 2 * width, half), BF16),
            pltpu.VMEM((SLOTS, width), BF16),
            pltpu.VMEM((SLOTS, width), BF16),
            pltpu.VMEM((SLOTS, width), BF16),
            pltpu.VMEM((count, width), F32),
            dma((2, PIECES)),
            dma((2, groups - 1)),
            dma((2, 1)),
            dma((2, HALVES, PLANE - 1)),
            dma((2, HALVES, DEPTH - 1)),
            dma((2, HALVES, DEPTH - 1)),
            dma((2, HALVES, PLANE - 1)),
        ],
        compiler_params=pltpu.CompilerParams(
            collective_id=0, has_side_effects=True, vmem_limit_bytes=48 * 2**20
        ),
    )(
        amplitudes, cycle_ints, int_rows, row_dest.T,
        vir_energy.reshape(1, width), occ_energy.reshape(count // 128, 128),
    )


def solution(mesh):
    fits = mesh.shape["pair"] == DEPTH * PLANE and mesh.shape["vir"] == 2
    return jax.shard_map(
        fused if fits else body,
        mesh=mesh,
        in_specs=(
            P("pair", "vir"),
            P("pair", "vir"),
            P("pair", "vir"),
            P("pair", None),
            P("vir"),
            P("pair"),
        ),
        out_specs=P("pair", "vir"),
        check_vma=False,
    )
```

```python
import math

import jax
import jax.numpy as jnp
from jax import lax
from jax.experimental import pallas as pl
from jax.experimental.pallas import tpu as pltpu
from jax.sharding import PartitionSpec as P

SLOTS = 256


def dispatch(int_rows, row_dest, groups, capacity):
    rows = int_rows.shape[0]
    group = jnp.arange(groups, dtype=jnp.int32)
    member = jnp.any(row_dest[None, :, :] == group[:, None, None], axis=2)
    before = jnp.arange(rows)[:, None] < jnp.arange(rows)[None, :]
    rank = jnp.dot(
        member.astype(jnp.bfloat16), before.astype(jnp.bfloat16), preferred_element_type=jnp.float32
    ).astype(jnp.int32)
    slot = jnp.arange(capacity, dtype=jnp.int32)
    select = member[:, None, :] & (rank[:, None, :] == slot[None, :, None])
    select = select.reshape(groups * capacity, rows).astype(int_rows.dtype)
    return jnp.dot(select, int_rows, preferred_element_type=jnp.float32).astype(int_rows.dtype)


def body(amplitudes, cycle_ints, int_rows, row_dest, vir_energy, occ_energy):
    groups = lax.axis_size("pair")
    row_count, local_width = amplitudes.shape
    full_width = local_width * lax.axis_size("vir")
    capacity = SLOTS // groups
    gathered = lax.all_gather(amplitudes, "vir", axis=1, tiled=True)
    cross_part = lax.dot_general(
        gathered, cycle_ints, (((0,), (0,)), ((), ())), preferred_element_type=jnp.float32
    )
    scale_cycle = math.sqrt(row_count * groups * full_width)
    cross_half = lax.psum((cross_part / scale_cycle).astype(jnp.bfloat16), "pair")
    outgoing = dispatch(int_rows, row_dest, groups, capacity)
    arrived = lax.all_to_all(
        outgoing.reshape(groups, capacity, local_width),
        "pair",
        split_axis=0,
        concat_axis=0,
        tiled=True,
    ).reshape(groups * capacity, local_width)
    chosen = lax.all_gather(arrived, "vir", axis=1, tiled=True)
    coefficient = lax.dot_general(
        gathered, chosen, (((1,), (1,)), ((), ())), preferred_element_type=jnp.float32
    ) / math.sqrt(full_width)
    ladder = jnp.dot(
        coefficient.astype(jnp.bfloat16), arrived, preferred_element_type=jnp.float32
    ) / math.sqrt(SLOTS)
    energy = (vir_energy[None, :] - occ_energy[:, None]) * amplitudes.astype(jnp.float32)
    cycle_term = jnp.dot(gathered, cross_half, preferred_element_type=jnp.float32)
    return (cycle_term + ladder + energy).astype(jnp.bfloat16)


DEPTH, PLANE, HALVES, PIECES = 4, 4, 2, 4
F32, BF16 = jnp.float32, jnp.bfloat16


def rows_at(start, size):
    return pl.ds(pl.multiple_of(start, size), size)


def kernel(
    amp_hbm, cyc_hbm, rows_hbm, dest_hbm, vir_hbm, occ_hbm, out,
    amp, cyc, rows, dest, vir_e, occ_e, other, part, plane_in, zsum, z_in, full, outgoing, arr, arr_o, acc,
    load_sem, amp_sem, route_sem, arr_sem, plane_sem, z_sem, gz_sem, gp_sem,
):
    groups = DEPTH * PLANE
    me, v = lax.axis_index("pair"), lax.axis_index("vir")
    z, q = me // PLANE, me % PLANE
    count, width = amp.shape
    full_width = 2 * width
    capacity = SLOTS // groups
    half = width // HALVES
    block = full_width // PLANE
    piece = block // DEPTH

    loads = [
        pltpu.make_async_copy(src, dst, load_sem.at[i])
        for i, (src, dst) in enumerate(
            (
                (dest_hbm, dest), (rows_hbm, rows), (vir_hbm, vir_e), (occ_hbm, occ_e),
                (amp_hbm, amp), (cyc_hbm, cyc),
            )
        )
    ]
    for c in loads:
        c.start()
    barrier = pltpu.get_barrier_semaphore()
    for k in range(1, groups):
        pl.semaphore_signal(
            barrier, inc=1, device_id=((me + k) % groups, v), device_id_type=pl.DeviceIdType.MESH
        )
    pl.semaphore_signal(barrier, inc=1, device_id=(me, 1 - v), device_id_type=pl.DeviceIdType.MESH)

    def copy(src, dst, sem, index, device):
        return pltpu.make_async_remote_copy(
            src_ref=src,
            dst_ref=dst,
            send_sem=sem.at[(0, *index)],
            recv_sem=sem.at[(1, *index)],
            device_id=device,
            device_id_type=pl.DeviceIdType.MESH,
        )

    loads[0].wait()
    loads[1].wait()
    group = lax.broadcasted_iota(jnp.int32, (SLOTS, rows.shape[0]), 0) // capacity
    slot = lax.broadcasted_iota(jnp.int32, (SLOTS, rows.shape[0]), 0) % capacity
    member = group == dest[0:1, :]
    for k in range(1, dest.shape[0]):
        member = member | (group == dest[k : k + 1, :])
    tri = (rows.shape[0], rows.shape[0])
    before = lax.broadcasted_iota(jnp.int32, tri, 0) < lax.broadcasted_iota(jnp.int32, tri, 1)
    rank = jnp.dot(
        jnp.where(member, 1.0, 0.0).astype(BF16),
        jnp.where(before, 1.0, 0.0).astype(BF16),
        preferred_element_type=F32,
    )
    select = jnp.where(member & (rank == slot.astype(F32)), 1.0, 0.0).astype(BF16)
    outgoing[...] = jnp.dot(select, rows[...], preferred_element_type=F32).astype(BF16)
    pl.semaphore_wait(barrier, groups)

    step = count // PIECES
    amp_copies = [
        copy(amp_hbm.at[pl.ds(i * step, step)], other.at[pl.ds(i * step, step)], amp_sem, (i,), (me, 1 - v))
        for i in range(PIECES)
    ]
    for c in amp_copies:
        c.start()
    route_copies = []
    for k in range(1, groups):
        to = (me + k) % groups
        c = copy(
            outgoing.at[rows_at(to * capacity, capacity)],
            arr.at[rows_at(me * capacity, capacity)],
            route_sem, (k - 1,), (to, v),
        )
        c.start()
        route_copies.append(c)
    mine = rows_at(me * capacity, capacity)
    arr[mine, :] = outgoing[mine, :]

    plane_copies = [
        [
            copy(
                part.at[h, rows_at((q + d) % PLANE * block, block)],
                plane_in.at[h, d - 1],
                plane_sem, (h, d - 1), (z * PLANE + (q + d) % PLANE, v),
            )
            for d in range(1, PLANE)
        ]
        for h in range(HALVES)
    ]

    def cross(src, owner, h):
        for j in range(width // block):
            value = lax.dot_general(
                src[:, pl.ds(j * block, block)],
                cyc[:, pl.ds(h * half, half)],
                (((0,), (0,)), ((), ())),
                preferred_element_type=F32,
            )
            part[h, rows_at(owner * width + j * block, block), :] = value.astype(BF16)
        for d in range(1, PLANE):
            target = (q + d) % PLANE

            @pl.when(target // (PLANE // 2) == owner)
            def _():
                plane_copies[h][d - 1].start()

    for c in loads[2:]:
        c.wait()
    for h in range(HALVES):
        cross(amp, v, h)
    for c in amp_copies:
        c.wait_recv()
    arr_copy = copy(arr, arr_o, arr_sem, (0,), (me, 1 - v))
    for h in range(HALVES):
        cross(other, 1 - v, h)
        if h == 0:
            for c in route_copies:
                c.wait_recv()
            arr_copy.start()
    tile = 256
    contract = (((1,), (1,)), ((), ()))

    def ladder(t, carry):
        at = rows_at(t * tile, tile)
        mine = amp[at, :]
        value = lax.dot_general(mine, arr[...], contract, preferred_element_type=F32)
        value += lax.dot_general(other[at, :], arr_o[...], contract, preferred_element_type=F32)
        value = (value / math.sqrt(full_width)).astype(BF16)
        value = jnp.dot(value, arr[...], preferred_element_type=F32) / math.sqrt(SLOTS)
        for s in range(tile // 128):
            line = jnp.broadcast_to(occ_e[pl.ds(t * (tile // 128) + s, 1), :], (128, 128)).T
            for b in range(width // 128):
                cols = slice(b * 128, (b + 1) * 128)
                sub = slice(s * 128, (s + 1) * 128)
                acc[pl.ds(pl.multiple_of(t * tile + s * 128, 128), 128), cols] = value[sub, cols] + (
                    vir_e[:, cols] - line
                ) * mine[sub, cols].astype(F32)
        return carry

    tiles = count // tile
    z_copies, gz_copies, gp_copies = [], [], []
    gp_h = [[] for _ in range(HALVES)]
    shares = 3 * HALVES - 1

    def some_ladder(i):
        lax.fori_loop(i * tiles // shares, (i + 1) * tiles // shares, ladder, 0)

    for h in range(HALVES):
        for c in plane_copies[h]:
            c.wait_recv()
        total = part[h, rows_at(q * block, block), :].astype(F32)
        for d in range(1, PLANE):
            total += plane_in[h, d - 1].astype(F32)
        zsum[h] = total.astype(BF16)
        for e in range(1, DEPTH):
            to = (z + e) % DEPTH
            c = copy(
                zsum.at[h, rows_at(to * piece, piece)],
                z_in.at[h, e - 1],
                z_sem, (h, e - 1), (to * PLANE + q, v),
            )
            c.start()
            z_copies.append(c)
        if h == 0:
            arr_copy.wait_recv()
        some_ladder(h)
    def spread(h, e):
        at = rows_at((q * DEPTH + (z - e + DEPTH) % DEPTH) * piece, piece)
        for d in range(1, PLANE):
            c = copy(
                full.at[h, at], full.at[h, at],
                gp_sem, (h, e, d - 1), (z * PLANE + (q + d) % PLANE, v),
            )
            c.start()
            gp_copies.append(c)
            gp_h[h].append(c)

    scale = math.sqrt(count * groups * full_width)
    own = rows_at((q * DEPTH + z) * piece, piece)
    for h in range(HALVES):
        for e in range(1, DEPTH):
            z_copies[h * (DEPTH - 1) + e - 1].wait_recv()
        total = zsum[h, rows_at(z * piece, piece), :].astype(F32)
        for e in range(1, DEPTH):
            total += z_in[h, e - 1].astype(F32)
        full[h, own, :] = (total / scale).astype(BF16)
        for e in range(1, DEPTH):
            c = copy(
                full.at[h, own], full.at[h, own], gz_sem, (h, e - 1), ((z + e) % DEPTH * PLANE + q, v)
            )
            c.start()
            gz_copies.append(c)
        spread(h, 0)
        some_ladder(HALVES + h)
    for h in range(HALVES):
        for e in range(1, DEPTH):
            gz_copies[h * (DEPTH - 1) + e - 1].wait_recv()
            spread(h, e)
        if h < HALVES - 1:
            some_ladder(2 * HALVES + h)
    for h in range(HALVES):
        for c in gp_h[h]:
            c.wait_recv()
        cols = slice(h * half, (h + 1) * half)

        def cycle(t, carry):
            at = rows_at(t * tile, tile)
            value = jnp.dot(
                amp[at, :], full[h, rows_at(v * width, width), :], preferred_element_type=F32
            )
            value += jnp.dot(
                other[at, :], full[h, rows_at((1 - v) * width, width), :], preferred_element_type=F32
            )
            out[at, cols] = (value + acc[at, cols]).astype(BF16)
            return carry

        lax.fori_loop(0, tiles, cycle, 0)
    plane_all = [c for part_of in plane_copies for c in part_of]
    for c in amp_copies + route_copies + [arr_copy] + plane_all + z_copies + gz_copies + gp_copies:
        c.wait_send()


def fused(amplitudes, cycle_ints, int_rows, row_dest, vir_energy, occ_energy):
    count, width = amplitudes.shape
    groups = DEPTH * PLANE
    half, block = width // HALVES, 2 * width // PLANE
    dma = pltpu.SemaphoreType.DMA
    return pl.pallas_call(
        kernel,
        out_shape=jax.ShapeDtypeStruct((count, width), BF16),
        in_specs=[pl.BlockSpec(memory_space=pl.ANY)] * 6,
        out_specs=pl.BlockSpec(memory_space=pltpu.VMEM),
        scratch_shapes=[
            pltpu.VMEM((count, width), BF16),
            pltpu.VMEM((count, width), BF16),
            pltpu.VMEM(int_rows.shape, BF16),
            pltpu.VMEM(row_dest.shape[::-1], jnp.int32),
            pltpu.VMEM((1, width), F32),
            pltpu.VMEM((count // 128, 128), F32),
            pltpu.VMEM((count, width), BF16),
            pltpu.VMEM((HALVES, 2 * width, half), BF16),
            pltpu.VMEM((HALVES, PLANE - 1, block, half), BF16),
            pltpu.VMEM((HALVES, block, half), BF16),
            pltpu.VMEM((HALVES, DEPTH - 1, block // DEPTH, half), BF16),
            pltpu.VMEM((HALVES, 2 * width, half), BF16),
            pltpu.VMEM((SLOTS, width), BF16),
            pltpu.VMEM((SLOTS, width), BF16),
            pltpu.VMEM((SLOTS, width), BF16),
            pltpu.VMEM((count, width), F32),
            dma((6,)),
            dma((2, PIECES)),
            dma((2, groups - 1)),
            dma((2, 1)),
            dma((2, HALVES, PLANE - 1)),
            dma((2, HALVES, DEPTH - 1)),
            dma((2, HALVES, DEPTH - 1)),
            dma((2, HALVES, DEPTH, PLANE - 1)),
        ],
        compiler_params=pltpu.CompilerParams(
            collective_id=0, has_side_effects=True, vmem_limit_bytes=60 * 2**20
        ),
    )(
        amplitudes, cycle_ints, int_rows, row_dest.T,
        vir_energy.reshape(1, width), occ_energy.reshape(count // 128, 128),
    )


def solution(mesh):
    fits = mesh.shape["pair"] == DEPTH * PLANE and mesh.shape["vir"] == 2
    return jax.shard_map(
        fused if fits else body,
        mesh=mesh,
        in_specs=(
            P("pair", "vir"),
            P("pair", "vir"),
            P("pair", "vir"),
            P("pair", None),
            P("vir"),
            P("pair"),
        ),
        out_specs=P("pair", "vir"),
        check_vma=False,
    )
```

```python
import math

import jax
import jax.numpy as jnp
from jax import lax
from jax.experimental import pallas as pl
from jax.experimental.pallas import tpu as pltpu
from jax.sharding import PartitionSpec as P

SLOTS = 256


def dispatch(int_rows, row_dest, groups, capacity):
    rows = int_rows.shape[0]
    group = jnp.arange(groups, dtype=jnp.int32)
    member = jnp.any(row_dest[None, :, :] == group[:, None, None], axis=2)
    before = jnp.arange(rows)[:, None] < jnp.arange(rows)[None, :]
    rank = jnp.dot(
        member.astype(jnp.bfloat16), before.astype(jnp.bfloat16), preferred_element_type=jnp.float32
    ).astype(jnp.int32)
    slot = jnp.arange(capacity, dtype=jnp.int32)
    select = member[:, None, :] & (rank[:, None, :] == slot[None, :, None])
    select = select.reshape(groups * capacity, rows).astype(int_rows.dtype)
    return jnp.dot(select, int_rows, preferred_element_type=jnp.float32).astype(int_rows.dtype)


def body(amplitudes, cycle_ints, int_rows, row_dest, vir_energy, occ_energy):
    groups = lax.axis_size("pair")
    row_count, local_width = amplitudes.shape
    full_width = local_width * lax.axis_size("vir")
    capacity = SLOTS // groups
    gathered = lax.all_gather(amplitudes, "vir", axis=1, tiled=True)
    cross_part = lax.dot_general(
        gathered, cycle_ints, (((0,), (0,)), ((), ())), preferred_element_type=jnp.float32
    )
    scale_cycle = math.sqrt(row_count * groups * full_width)
    cross_half = lax.psum((cross_part / scale_cycle).astype(jnp.bfloat16), "pair")
    outgoing = dispatch(int_rows, row_dest, groups, capacity)
    arrived = lax.all_to_all(
        outgoing.reshape(groups, capacity, local_width),
        "pair",
        split_axis=0,
        concat_axis=0,
        tiled=True,
    ).reshape(groups * capacity, local_width)
    chosen = lax.all_gather(arrived, "vir", axis=1, tiled=True)
    coefficient = lax.dot_general(
        gathered, chosen, (((1,), (1,)), ((), ())), preferred_element_type=jnp.float32
    ) / math.sqrt(full_width)
    ladder = jnp.dot(
        coefficient.astype(jnp.bfloat16), arrived, preferred_element_type=jnp.float32
    ) / math.sqrt(SLOTS)
    energy = (vir_energy[None, :] - occ_energy[:, None]) * amplitudes.astype(jnp.float32)
    cycle_term = jnp.dot(gathered, cross_half, preferred_element_type=jnp.float32)
    return (cycle_term + ladder + energy).astype(jnp.bfloat16)


DEPTH, PLANE, HALVES, PIECES = 4, 4, 2, 4
F32, BF16 = jnp.float32, jnp.bfloat16


def rows_at(start, size):
    return pl.ds(pl.multiple_of(start, size), size)


def kernel(
    amp_hbm, cyc_hbm, rows_hbm, dest_hbm, vir_hbm, occ_hbm, out,
    amp, cyc, rows, dest, vir_e, occ_e, other, part, plane_in, zsum, z_in, full, outgoing, arr, arr_o, acc,
    load_sem, amp_sem, route_sem, arr_sem, plane_sem, z_sem, gz_sem, gp_sem,
):
    groups = DEPTH * PLANE
    me, v = lax.axis_index("pair"), lax.axis_index("vir")
    z, q = me // PLANE, me % PLANE
    count, width = amp.shape
    full_width = 2 * width
    capacity = SLOTS // groups
    half = width // HALVES
    block = full_width // PLANE
    piece = block // DEPTH

    loads = [
        pltpu.make_async_copy(src, dst, load_sem.at[i])
        for i, (src, dst) in enumerate(
            (
                (dest_hbm, dest), (rows_hbm, rows), (vir_hbm, vir_e), (occ_hbm, occ_e),
                (amp_hbm, amp), (cyc_hbm, cyc),
            )
        )
    ]
    for c in loads:
        c.start()
    barrier = pltpu.get_barrier_semaphore()
    for k in range(1, groups):
        pl.semaphore_signal(
            barrier, inc=1, device_id=((me + k) % groups, v), device_id_type=pl.DeviceIdType.MESH
        )
    pl.semaphore_signal(barrier, inc=1, device_id=(me, 1 - v), device_id_type=pl.DeviceIdType.MESH)

    def copy(src, dst, sem, index, device):
        return pltpu.make_async_remote_copy(
            src_ref=src,
            dst_ref=dst,
            send_sem=sem.at[(0, *index)],
            recv_sem=sem.at[(1, *index)],
            device_id=device,
            device_id_type=pl.DeviceIdType.MESH,
        )

    loads[0].wait()
    loads[1].wait()
    group = lax.broadcasted_iota(jnp.int32, (SLOTS, rows.shape[0]), 0) // capacity
    slot = lax.broadcasted_iota(jnp.int32, (SLOTS, rows.shape[0]), 0) % capacity
    member = group == dest[0:1, :]
    for k in range(1, dest.shape[0]):
        member = member | (group == dest[k : k + 1, :])
    tri = (rows.shape[0], rows.shape[0])
    before = lax.broadcasted_iota(jnp.int32, tri, 0) < lax.broadcasted_iota(jnp.int32, tri, 1)
    rank = jnp.dot(
        jnp.where(member, 1.0, 0.0).astype(BF16),
        jnp.where(before, 1.0, 0.0).astype(BF16),
        preferred_element_type=F32,
    )
    select = jnp.where(member & (rank == slot.astype(F32)), 1.0, 0.0).astype(BF16)
    outgoing[...] = jnp.dot(select, rows[...], preferred_element_type=F32).astype(BF16)
    pl.semaphore_wait(barrier, groups)

    step = count // PIECES
    amp_copies = [
        copy(amp_hbm.at[pl.ds(i * step, step)], other.at[pl.ds(i * step, step)], amp_sem, (i,), (me, 1 - v))
        for i in range(PIECES)
    ]
    for c in amp_copies:
        c.start()
    route_copies = []
    for k in range(1, groups):
        to = (me + k) % groups
        c = copy(
            outgoing.at[rows_at(to * capacity, capacity)],
            arr.at[rows_at(me * capacity, capacity)],
            route_sem, (k - 1,), (to, v),
        )
        c.start()
        route_copies.append(c)
    mine = rows_at(me * capacity, capacity)
    arr[mine, :] = outgoing[mine, :]

    plane_copies = [
        [
            [
                copy(
                    part.at[h, rows_at(((q + d) % PLANE * DEPTH + (z + e) % DEPTH) * piece, piece)],
                    plane_in.at[h, d - 1, rows_at((z + e) % DEPTH * piece, piece)],
                    plane_sem, (h, e % DEPTH, d - 1), (z * PLANE + (q + d) % PLANE, v),
                )
                for e in range(1, DEPTH + 1)
            ]
            for d in range(1, PLANE)
        ]
        for h in range(HALVES)
    ]

    def cross(src, owner, h):
        for j in range(width // block):
            value = lax.dot_general(
                src[:, pl.ds(j * block, block)],
                cyc[:, pl.ds(h * half, half)],
                (((0,), (0,)), ((), ())),
                preferred_element_type=F32,
            )
            part[h, rows_at(owner * width + j * block, block), :] = value.astype(BF16)
        for d in range(1, PLANE):
            target = (q + d) % PLANE

            @pl.when(target // (PLANE // 2) == owner)
            def _():
                for c in plane_copies[h][d - 1]:
                    c.start()

    for c in loads[2:]:
        c.wait()
    for h in range(HALVES):
        cross(amp, v, h)
    for c in amp_copies:
        c.wait_recv()
    arr_copy = copy(arr, arr_o, arr_sem, (0,), (me, 1 - v))
    for h in range(HALVES):
        cross(other, 1 - v, h)
        if h == 0:
            for c in route_copies:
                c.wait_recv()
            arr_copy.start()
    tile = 256
    contract = (((1,), (1,)), ((), ()))

    def ladder(t, carry):
        at = rows_at(t * tile, tile)
        mine = amp[at, :]
        value = lax.dot_general(mine, arr[...], contract, preferred_element_type=F32)
        value += lax.dot_general(other[at, :], arr_o[...], contract, preferred_element_type=F32)
        value = (value / math.sqrt(full_width)).astype(BF16)
        value = jnp.dot(value, arr[...], preferred_element_type=F32) / math.sqrt(SLOTS)
        for s in range(tile // 128):
            line = jnp.broadcast_to(occ_e[pl.ds(t * (tile // 128) + s, 1), :], (128, 128)).T
            for b in range(width // 128):
                cols = slice(b * 128, (b + 1) * 128)
                sub = slice(s * 128, (s + 1) * 128)
                acc[pl.ds(pl.multiple_of(t * tile + s * 128, 128), 128), cols] = value[sub, cols] + (
                    vir_e[:, cols] - line
                ) * mine[sub, cols].astype(F32)
        return carry

    tiles = count // tile
    z_copies, gz_copies, gp_copies = [], [], []
    gp_h = [[] for _ in range(HALVES)]
    shares = 3 * HALVES - 1

    def some_ladder(i):
        lax.fori_loop(i * tiles // shares, (i + 1) * tiles // shares, ladder, 0)

    for h in range(HALVES):
        for e in range(1, DEPTH + 1):
            to = (z + e) % DEPTH
            for d in range(1, PLANE):
                plane_copies[h][d - 1][e - 1].wait_recv()
            at = rows_at(to * piece, piece)
            total = part[h, rows_at((q * DEPTH + to) * piece, piece), :].astype(F32)
            for d in range(1, PLANE):
                total += plane_in[h, d - 1, at, :].astype(F32)
            zsum[h, at, :] = total.astype(BF16)
            if e < DEPTH:
                c = copy(
                    zsum.at[h, at], z_in.at[h, e - 1], z_sem, (h, e - 1), (to * PLANE + q, v)
                )
                c.start()
                z_copies.append(c)
        if h == 0:
            arr_copy.wait_recv()
        some_ladder(h)
    def spread(h, e):
        at = rows_at((q * DEPTH + (z - e + DEPTH) % DEPTH) * piece, piece)
        for d in range(1, PLANE):
            c = copy(
                full.at[h, at], full.at[h, at],
                gp_sem, (h, e, d - 1), (z * PLANE + (q + d) % PLANE, v),
            )
            c.start()
            gp_copies.append(c)
            gp_h[h].append(c)

    scale = math.sqrt(count * groups * full_width)
    own = rows_at((q * DEPTH + z) * piece, piece)
    for h in range(HALVES):
        for e in range(1, DEPTH):
            z_copies[h * (DEPTH - 1) + e - 1].wait_recv()
        total = zsum[h, rows_at(z * piece, piece), :].astype(F32)
        for e in range(1, DEPTH):
            total += z_in[h, e - 1].astype(F32)
        full[h, own, :] = (total / scale).astype(BF16)
        for e in range(1, DEPTH):
            c = copy(
                full.at[h, own], full.at[h, own], gz_sem, (h, e - 1), ((z + e) % DEPTH * PLANE + q, v)
            )
            c.start()
            gz_copies.append(c)
        spread(h, 0)
        some_ladder(HALVES + h)
    for h in range(HALVES):
        for e in range(1, DEPTH):
            gz_copies[h * (DEPTH - 1) + e - 1].wait_recv()
            spread(h, e)
        if h < HALVES - 1:
            some_ladder(2 * HALVES + h)
    for h in range(HALVES):
        for c in gp_h[h]:
            c.wait_recv()
        cols = slice(h * half, (h + 1) * half)

        def cycle(t, carry):
            at = rows_at(t * tile, tile)
            value = jnp.dot(
                amp[at, :], full[h, rows_at(v * width, width), :], preferred_element_type=F32
            )
            value += jnp.dot(
                other[at, :], full[h, rows_at((1 - v) * width, width), :], preferred_element_type=F32
            )
            out[at, cols] = (value + acc[at, cols]).astype(BF16)
            return carry

        lax.fori_loop(0, tiles, cycle, 0)
    plane_all = [c for of_half in plane_copies for of_peer in of_half for c in of_peer]
    for c in amp_copies + route_copies + [arr_copy] + plane_all + z_copies + gz_copies + gp_copies:
        c.wait_send()


def fused(amplitudes, cycle_ints, int_rows, row_dest, vir_energy, occ_energy):
    count, width = amplitudes.shape
    groups = DEPTH * PLANE
    half, block = width // HALVES, 2 * width // PLANE
    dma = pltpu.SemaphoreType.DMA
    return pl.pallas_call(
        kernel,
        out_shape=jax.ShapeDtypeStruct((count, width), BF16),
        in_specs=[pl.BlockSpec(memory_space=pl.ANY)] * 6,
        out_specs=pl.BlockSpec(memory_space=pltpu.VMEM),
        scratch_shapes=[
            pltpu.VMEM((count, width), BF16),
            pltpu.VMEM((count, width), BF16),
            pltpu.VMEM(int_rows.shape, BF16),
            pltpu.VMEM(row_dest.shape[::-1], jnp.int32),
            pltpu.VMEM((1, width), F32),
            pltpu.VMEM((count // 128, 128), F32),
            pltpu.VMEM((count, width), BF16),
            pltpu.VMEM((HALVES, 2 * width, half), BF16),
            pltpu.VMEM((HALVES, PLANE - 1, block, half), BF16),
            pltpu.VMEM((HALVES, block, half), BF16),
            pltpu.VMEM((HALVES, DEPTH - 1, block // DEPTH, half), BF16),
            pltpu.VMEM((HALVES, 2 * width, half), BF16),
            pltpu.VMEM((SLOTS, width), BF16),
            pltpu.VMEM((SLOTS, width), BF16),
            pltpu.VMEM((SLOTS, width), BF16),
            pltpu.VMEM((count, width), F32),
            dma((6,)),
            dma((2, PIECES)),
            dma((2, groups - 1)),
            dma((2, 1)),
            dma((2, HALVES, DEPTH, PLANE - 1)),
            dma((2, HALVES, DEPTH - 1)),
            dma((2, HALVES, DEPTH - 1)),
            dma((2, HALVES, DEPTH, PLANE - 1)),
        ],
        compiler_params=pltpu.CompilerParams(
            collective_id=0, has_side_effects=True, vmem_limit_bytes=60 * 2**20
        ),
    )(
        amplitudes, cycle_ints, int_rows, row_dest.T,
        vir_energy.reshape(1, width), occ_energy.reshape(count // 128, 128),
    )


def solution(mesh):
    fits = mesh.shape["pair"] == DEPTH * PLANE and mesh.shape["vir"] == 2
    return jax.shard_map(
        fused if fits else body,
        mesh=mesh,
        in_specs=(
            P("pair", "vir"),
            P("pair", "vir"),
            P("pair", "vir"),
            P("pair", None),
            P("vir"),
            P("pair"),
        ),
        out_specs=P("pair", "vir"),
        check_vma=False,
    )
```
